32 devices in a mesh: ta: 8 (over y, x, core), sa: 4 (over z).
Axes of the slice: x: 2, y: 2, z: 4, core: 2. Of those that a mesh axis runs over, the one named last changes fastest.
Arguments:
- null_vectors: bfloat16 [2, 24, 4, 3, 32, 16, 128], P(None, None, None, None, 'ta', 'sa'), may hold values from -0.15234375 to 0.15234375
- gauge_links: bfloat16 [2, 4, 3, 3, 32, 16, 128], P(None, None, None, None, 'ta', 'sa'), may hold values from -3.59375 to 3.59375
- coarse_in: float32 [8, 4, 8, 96], P('ta', 'sa'), may hold values from -6 to 6
Outputs:
- coarse_links: float32 [8, 4, 8, 5, 4608], P('ta', 'sa')
- coarse_out: float32 [8, 4, 8, 96], P('ta', 'sa')
The draws below stay inside these ranges and needn't reach their ends.
All inputs are finite; a program needn't handle non-finite values.
Results may differ from the reference program's by a relative error of at most 0.0018.
Values may be sent and summed in bfloat16 or wider, within the bound.
A program may use at most 256 MiB of HBM per device.

```python
import jax
import jax.numpy as jnp
from jax import lax

LAT_Y = 4
LAT_X = 32
NVEC = 24
LAT_T = 32
LAT_Z = 16
PLANE = 128
AGG_T = 8
AGG_Z = 4
AGG_Y = 1
AGG_X = 8
APLANE = 8
NCOL = 48
BLOCK = 4608


def levels(key, extent, pieces, smallest, top_value):
    gain = 1.0
    for position, shards_of in pieces:
        heights = jax.random.uniform(jax.random.fold_in(jax.random.fold_in(key, 6), position), (shards_of,), jnp.float32, smallest / len(pieces), top_value / len(pieces))
        gain = gain * jnp.repeat(jnp.exp(heights), extent[position] // shards_of).reshape((-1,) + (1,) * (len(extent) - 1 - position))
    return gain


def bell_draw(own_key, shape, scale, bound, cuts=(), kind=jnp.bfloat16):
    array = jax.random.normal(own_key, shape, jnp.float32) * scale
    if len(cuts) > 0:
        array = levels(own_key, shape, cuts, -0.22, 0.18) * array
    return jnp.clip(array, min=-bound, max=bound).astype(kind)


def setup_inputs(seed: int = 0) -> dict:
    splits = jax.random.split(jax.random.key(seed), 4)
    return {
        "null_vectors": bell_draw(splits[0], (2, NVEC, 4, 3, LAT_T, LAT_Z, PLANE), 0.0255, 0.15234375, ((4, 8), (5, 4))),
        "gauge_links": bell_draw(splits[1], (2, 4, 3, 3, LAT_T, LAT_Z, PLANE), 0.6, 3.59375, ((4, 8), (5, 4))),
        "coarse_in": bell_draw(splits[2], (AGG_T, AGG_Z, APLANE, 2 * NCOL), 1.0, 6.0, ((0, 8), (1, 4)), jnp.float32),
    }


gamma_rows = (
    ((2, 1.0, 0.0), (3, 1.0, 0.0), (0, 1.0, 0.0), (1, 1.0, 0.0)),
    ((2, 0.0, -1.0), (3, 0.0, 1.0), (0, 0.0, 1.0), (1, 0.0, -1.0)),
    ((3, -1.0, 0.0), (2, 1.0, 0.0), (1, 1.0, 0.0), (0, -1.0, 0.0)),
    ((3, 0.0, -1.0), (2, 0.0, -1.0), (1, 0.0, 1.0), (0, 0.0, 1.0)),
)
diag_shift = 1.0


def color_product(link_field, vectors):
    real_part = 0.0
    imag_part = 0.0
    for colour in range(3):
        link_r = link_field[0, :, colour][None, None].astype(jnp.float32)
        link_i = link_field[1, :, colour][None, None].astype(jnp.float32)
        vector_r = vectors[0, :, :, colour][:, :, None].astype(jnp.float32)
        vector_i = vectors[1, :, :, colour][:, :, None].astype(jnp.float32)
        real_part = real_part + link_r * vector_r - link_i * vector_i
        imag_part = imag_part + link_r * vector_i + link_i * vector_r
    return real_part, imag_part


def hop_terms(real_part, imag_part, direction):
    same_hop = jnp.stack([-0.5 * real_part, -0.5 * imag_part]).astype(jnp.bfloat16)
    rows_real = []
    rows_imag = []
    for spin in range(4):
        source, phase_r, phase_i = gamma_rows[direction][spin]
        rows_real.append(phase_r * real_part[:, source] - phase_i * imag_part[:, source])
        rows_imag.append(phase_r * imag_part[:, source] + phase_i * real_part[:, source])
    cross_hop = (0.5 * jnp.stack([jnp.stack(rows_real, 1), jnp.stack(rows_imag, 1)])).astype(jnp.bfloat16)
    return same_hop, cross_hop


def blocked(field):
    field_shape = field.shape
    return field.reshape(field_shape[:4] + (field_shape[4] // 4, 4, field_shape[5] // 4, 4, LAT_Y // 4, 4, LAT_X // 4, 4))


def pair_product(left_side, right_side):
    return jnp.einsum('rvscTaZbYdXe,qwscTaZbYdXe->TZYXrvqw', left_side.astype(jnp.float32),
                      right_side.astype(jnp.float32), precision=lax.Precision.HIGHEST)


def contract(vectors, same_hop, cross_hop):
    vector_count = vectors.shape[1]
    hops = jnp.concatenate([same_hop, cross_hop], axis=1)
    row_blocks = []
    for chirality in range(2):
        spin_range = slice(2 * chirality, 2 * chirality + 2)
        product = pair_product(vectors[:, :, spin_range], hops[:, :, spin_range])
        real_part = product[..., 0, :, 0, :] + product[..., 1, :, 1, :]
        imag_part = product[..., 0, :, 1, :] - product[..., 1, :, 0, :]
        components = []
        for component in (real_part, imag_part):
            same_cols = component[..., :vector_count]
            cross_cols = component[..., vector_count:]
            if chirality == 0:
                components.append(jnp.concatenate([same_cols, cross_cols], axis=-1))
            else:
                components.append(jnp.concatenate([cross_cols, same_cols], axis=-1))
        row_blocks.append(jnp.stack(components, axis=-3))
    return jnp.concatenate(row_blocks, axis=-2)


def gram(vectors):
    row_blocks = []
    for chirality in range(2):
        spin_range = slice(2 * chirality, 2 * chirality + 2)
        product = pair_product(vectors[:, :, spin_range], vectors[:, :, spin_range])
        real_part = product[..., 0, :, 0, :] + product[..., 1, :, 1, :]
        imag_part = product[..., 0, :, 1, :] - product[..., 1, :, 0, :]
        components = []
        for component in (real_part, imag_part):
            zero_block = jnp.zeros_like(component)
            if chirality == 0:
                components.append(jnp.concatenate([component, zero_block], axis=-1))
            else:
                components.append(jnp.concatenate([zero_block, component], axis=-1))
        row_blocks.append(jnp.stack(components, axis=-3))
    return jnp.concatenate(row_blocks, axis=-2)


def adjoint(blocks):
    vector_count = blocks.shape[-1] // 2
    chirality_sign = jnp.concatenate([jnp.ones(vector_count, jnp.float32), -jnp.ones(vector_count, jnp.float32)])
    outer_sign = chirality_sign[:, None] * chirality_sign[None, :]
    real_part = outer_sign * jnp.swapaxes(blocks[..., 0, :, :], -1, -2)
    imag_part = -outer_sign * jnp.swapaxes(blocks[..., 1, :, :], -1, -2)
    return jnp.stack([real_part, imag_part], axis=-3)


def neighbour(field, direction):
    if direction == 1:
        return jnp.roll(field, -1, axis=5)
    plane_field = field.reshape(field.shape[:6] + (LAT_Y, LAT_X))
    plane_field = jnp.roll(plane_field, -1, axis=6 if direction == 2 else 7)
    return plane_field.reshape(field.shape)


def slab_links(vectors, next_slice, gauge_slab):
    blocked_vectors = blocked(vectors)
    diagonal = diag_shift * gram(blocked_vectors)
    forward_links = []
    for direction in range(4):
        if direction == 0:
            shifted = jnp.concatenate([vectors[:, :, :, :, 1:], next_slice], axis=4)
        else:
            shifted = neighbour(vectors, direction)
        real_part, imag_part = color_product(gauge_slab[:, direction], shifted)
        same_hop, cross_hop = hop_terms(real_part, imag_part, direction)
        same_view = blocked(same_hop)
        cross_view = blocked(cross_hop)
        local_axis = 5 + 2 * direction
        inner_part = contract(lax.slice_in_dim(blocked_vectors, 0, 3, axis=local_axis),
                              lax.slice_in_dim(same_view, 0, 3, axis=local_axis),
                              lax.slice_in_dim(cross_view, 0, 3, axis=local_axis))
        outer_part = contract(lax.slice_in_dim(blocked_vectors, 3, 4, axis=local_axis),
                              lax.slice_in_dim(same_view, 3, 4, axis=local_axis),
                              lax.slice_in_dim(cross_view, 3, 4, axis=local_axis))
        diagonal = diagonal + inner_part + adjoint(inner_part)
        forward_links.append(outer_part)
    return jnp.stack([diagonal] + forward_links, axis=-4)


def matvec(blocks, coarse_vector):
    def times_vector(matrix, column):
        return jnp.einsum('...ij,...j->...i', matrix, column, precision=lax.Precision.HIGHEST)
    real_part = times_vector(blocks[..., 0, :, :], coarse_vector[..., 0, :]) - times_vector(blocks[..., 1, :, :], coarse_vector[..., 1, :])
    imag_part = times_vector(blocks[..., 0, :, :], coarse_vector[..., 1, :]) + times_vector(blocks[..., 1, :, :], coarse_vector[..., 0, :])
    return jnp.stack([real_part, imag_part], axis=-2)


def coarse_apply(coarse_blocks, coarse_vector):
    result = matvec(coarse_blocks[..., 0, :, :, :], coarse_vector)
    for direction in range(4):
        link_block = coarse_blocks[..., 1 + direction, :, :, :]
        result = result + matvec(link_block, jnp.roll(coarse_vector, -1, axis=direction))
        result = result + jnp.roll(matvec(adjoint(link_block), coarse_vector), 1, axis=direction)
    return result


def reference(null_vectors, gauge_links, coarse_in):
    def one_slab(slab_index):
        first_slice = (slab_index * 4).astype(jnp.int32)
        vectors = lax.dynamic_slice_in_dim(null_vectors, first_slice, 4, axis=4)
        following = ((first_slice + 4) % LAT_T).astype(jnp.int32)
        next_slice = lax.dynamic_slice_in_dim(null_vectors, following, 1, axis=4)
        gauge_slab = lax.dynamic_slice_in_dim(gauge_links, first_slice, 4, axis=4)
        return slab_links(vectors, next_slice, gauge_slab)[0]

    coarse_blocks = lax.map(one_slab, jnp.arange(AGG_T, dtype=jnp.int32))
    coarse_vector = coarse_in.reshape(AGG_T, AGG_Z, AGG_Y, AGG_X, 2, NCOL)
    once_applied = coarse_apply(coarse_blocks, coarse_vector)
    twice_applied = coarse_apply(coarse_blocks, once_applied)
    return (coarse_blocks.reshape(AGG_T, AGG_Z, APLANE, 5, BLOCK),
            twice_applied.reshape(AGG_T, AGG_Z, APLANE, 2 * NCOL))
```

```python
import functools

import jax
import jax.numpy as jnp
from jax import lax
from jax.experimental import pallas as pl
from jax.experimental.pallas import tpu as pltpu
from jax.sharding import PartitionSpec as P

LAT_X = 32
MESH = pl.DeviceIdType.MESH

SOURCE = ((2, 3, 0, 1), (2, 3, 0, 1), (3, 2, 1, 0), (3, 2, 1, 0))
ODD_SIGN = (False, True, True, False)
PHASE = ((0, 0), (3, 1), (2, 0), (3, 1))


def turn(re, im, power):
    if power == 0:
        return re, im
    if power == 1:
        return -im, re
    if power == 2:
        return -re, -im
    return im, -re


def hop_rows(same, cross, chi):
    first, second = (same, cross) if chi == 0 else (cross, same)
    of_real = jnp.concatenate([first[0], second[0], first[1], second[1]], 0)
    of_imag = jnp.concatenate([first[1], second[1], -first[0], -second[0]], 0)
    return of_real.astype(jnp.bfloat16), of_imag.astype(jnp.bfloat16)


def place_hops(direction, slot, shifted, u_ref, tz, right):
    links = []
    for q in range(2):
        links.append([[u_ref[tz, pl.ds(((q * 4 + direction) * 3 + row) * 3 + col, 1), :]
                       for col in range(3)] for row in range(3)])
    for c in range(3):
        hops = []
        for s in range(4):
            re = None
            im = None
            for d in range(3):
                lr, li = links[0][c][d], links[1][c][d]
                vr, vi = shifted[s][d]
                term_r = lr * vr - li * vi
                term_i = lr * vi + li * vr
                re = term_r if re is None else re + term_r
                im = term_i if im is None else im + term_i
            hops.append((re, im))
        for s in range(4):
            chi = s // 2
            same = (-hops[s][0], -hops[s][1])
            power = PHASE[direction][chi]
            if ODD_SIGN[direction] and s % 2 == 1:
                power = (power + 2) % 4
            cross = turn(*hops[SOURCE[direction][s]], power)
            of_real, of_imag = hop_rows(same, cross, chi)
            k = (s % 2) * 3 + c
            right[chi, 96 * slot:96 * slot + 96, 128 * k:128 * k + 128] = of_real
            right[chi, 96 * slot:96 * slot + 96, 128 * (k + 6):128 * (k + 7)] = of_imag


def place_left(values, mask_ref, left):
    copies = mask_ref.shape[0] // 48
    for s in range(4):
        for c in range(3):
            for q in range(2):
                part = values[s][c][q]
                twice = jnp.concatenate([part, part], 0).astype(jnp.bfloat16)
                k = q * 6 + (s % 2) * 3 + c
                for i in range(copies):
                    rows = slice(48 * i, 48 * i + 48)
                    left[s // 2, rows, 128 * k:128 * k + 128] = twice * mask_ref[rows, :]


def masks(mask_ref):
    rows = lax.broadcasted_iota(jnp.int32, mask_ref.shape, 0)
    lanes = lax.broadcasted_iota(jnp.int32, mask_ref.shape, 1)
    kind = rows // 192
    aggregate = rows % 192 // 24
    own = (lanes % LAT_X) // 4 == aggregate
    y_edge = lanes // LAT_X % 4 == 3
    x_edge = lanes % 4 == 3
    keep = own & ((kind == 0) | ((kind == 1) & y_edge) | ((kind == 2) & x_edge))
    mask_ref[...] = jnp.where(keep, 1.0, 0.0).astype(jnp.bfloat16)


def load(read):
    out = []
    for s in range(4):
        row = []
        for c in range(3):
            whole = read(s, c).astype(jnp.float32)
            row.append((whole[:24], whole[24:]))
        out.append(row)
    return out


def product(left, right):
    return lax.dot_general(left, right, (((1,), (1,)), ((), ())), preferred_element_type=jnp.float32)


def plane_kernel(v_ref, u_ref, sums, mask, left, right):
    masks(mask)
    sums[...] = jnp.zeros_like(sums)
    lane = lax.broadcasted_iota(jnp.int32, (24, 128), 1)
    wraps = lane % LAT_X == LAT_X - 1

    @pl.loop(0, v_ref.shape[0])
    def _(tz):
        values = load(lambda s, c: v_ref[tz, s, c])
        place_left(values, mask, left)
        for s in range(4):
            for c in range(3):
                vr, vi = values[s][c]
                k = (s % 2) * 3 + c
                right[s // 2, 192:240, 128 * k:128 * k + 128] = (
                    jnp.concatenate([vr, vi], 0).astype(jnp.bfloat16))
                right[s // 2, 192:240, 128 * (k + 6):128 * (k + 7)] = (
                    jnp.concatenate([vi, -vr], 0).astype(jnp.bfloat16))

        def ahead_y(part):
            return pltpu.roll(part, 128 - LAT_X, 1)

        def ahead_x(part):
            return jnp.where(wraps, pltpu.roll(part, LAT_X - 1, 1), pltpu.roll(part, 127, 1))

        for slot, (direction, move) in enumerate(((2, ahead_y), (3, ahead_x))):
            shifted = [[(move(values[s][c][0]), move(values[s][c][1])) for c in range(3)] for s in range(4)]
            place_hops(direction, slot, shifted, u_ref, tz, right)
        for chi in range(2):
            sums[chi] += product(left[chi], right[chi])


def line_kernel(v_ref, u_ref, face_t, face_z, plane_sums, blocks, mask, left, right, sums, held):
    masks(mask)
    sums[...] = jnp.zeros_like(sums)

    @pl.loop(0, v_ref.shape[0])
    def _(tz):
        t = tz // 4
        z = tz % 4

        @pl.when(t < 3)
        def _():
            held[0] = v_ref[jnp.minimum(tz + 4, 15)]

        @pl.when(t == 3)
        def _():
            held[0] = face_t[z]

        @pl.when(z < 3)
        def _():
            held[1] = v_ref[jnp.minimum(tz + 1, 15)]

        @pl.when(z == 3)
        def _():
            held[1] = face_z[t]

        values = load(lambda s, c: v_ref[tz, s, c])
        place_left(values, mask, left)
        for direction in range(2):
            shifted = load(lambda s, c: held[direction, s, c])
            place_hops(direction, direction, shifted, u_ref, tz, right)
        kind = jnp.where(t == 3, 2, 0) + jnp.where(z == 3, 1, 0)
        for chi in range(2):
            sums[kind, chi] += product(left[chi], right[chi])

    row = lax.broadcasted_iota(jnp.int32, (48, 48), 0)
    col = lax.broadcasted_iota(jnp.int32, (48, 48), 1)
    sign = jnp.where((row < 24) == (col < 24), 1.0, -1.0)
    zero = jnp.zeros((24, 24), jnp.float32)
    for a in range(8):
        parts = [[], [], [], [], []]
        for chi in range(2):
            rows = slice(24 * a, 24 * a + 24)
            k0, k1, k2, k3 = [sums[kind, chi, rows, :] for kind in range(4)]
            whole = plane_sums[chi, rows, :]
            y_out = plane_sums[chi, 192 + 24 * a:216 + 24 * a, 0:96]
            x_out = plane_sums[chi, 384 + 24 * a:408 + 24 * a, 96:192]
            t_out = (k2 + k3)[:, 0:96]
            z_out = (k1 + k3)[:, 96:192]
            inner = (k0 + k1)[:, 0:96] + (k0 + k2)[:, 96:192]
            inner = inner + (whole[:, 0:96] - y_out) + (whole[:, 96:192] - x_out)
            g_re, g_im = whole[:, 192:216], whole[:, 216:240]
            gram = [g_re, zero, g_im, zero] if chi == 0 else [zero, g_re, zero, g_im]
            for i, part in enumerate((inner, t_out, z_out, y_out, x_out)):
                parts[i].append(part)
            parts[0][chi] = (inner, jnp.concatenate(gram, 1))
        inner = jnp.concatenate([parts[0][0][0], parts[0][1][0]], 0)
        gram = jnp.concatenate([parts[0][0][1], parts[0][1][1]], 0)
        adj = jnp.concatenate([sign * inner[:, :48].T, -sign * inner[:, 48:].T], 1)
        blocks[a, 0] = gram + inner + adj
        for i in range(1, 5):
            blocks[a, i] = jnp.concatenate(parts[i], 0)


def coarse_kernel(axes, blocks, phi_ref, out_ref, phi, ahead, back, got, send, recv):
    counts = [lax.axis_size(name) for name in axes]
    here = [lax.axis_index(name) for name in axes]

    def target(axis, step):
        spot = list(here)
        spot[axis] = lax.rem(here[axis] + step + counts[axis], counts[axis])
        return tuple(spot)

    barrier = pltpu.get_barrier_semaphore()
    for axis in range(2):
        for step in (-1, 1):
            pl.semaphore_signal(barrier, inc=1, device_id=target(axis, step), device_id_type=MESH)
    pl.semaphore_wait(barrier, 4)

    lane = lax.broadcasted_iota(jnp.int32, (1, 96), 1)
    row48 = lax.broadcasted_iota(jnp.int32, (48, 96), 0)
    lane48 = lax.broadcasted_iota(jnp.int32, (48, 96), 1)
    first = lane < 48
    gamma_row = jnp.where(lane % 48 < 24, 1.0, -1.0)
    gamma_col = jnp.where(lax.broadcasted_iota(jnp.int32, (48, 1), 0) < 24, 1.0, -1.0)
    eye_re = jnp.where(row48 == lane48, 1.0, 0.0)
    eye_im = jnp.where(row48 + 48 == lane48, 1.0, 0.0)

    def swapped(vector):
        return jnp.concatenate([vector[:, 48:], vector[:, :48]], 1)

    def forward(block, vector):
        other = swapped(vector)
        return block * jnp.where(first, vector, -vector), block * other

    def columns(vector):
        re = jnp.sum(vector * eye_re, 1, keepdims=True) * gamma_col
        im = jnp.sum(vector * eye_im, 1, keepdims=True) * gamma_col
        return re, im

    def backward(block, cols):
        re = jnp.sum(block * cols[0], 0, keepdims=True)
        im = jnp.sum(block * cols[1], 0, keepdims=True)
        other_im = swapped(im)
        return gamma_row * jnp.where(first, re + other_im, other_im - re)

    def copy(step, kind, src, dst, to):
        return pltpu.make_async_remote_copy(
            src_ref=src, dst_ref=dst, send_sem=send.at[step, kind], recv_sem=recv.at[step, kind],
            device_id=to, device_id_type=MESH)

    phi[0] = phi_ref[...]
    for step in range(2):
        copies = []
        for axis in range(2):
            copies.append(copy(step, axis, phi.at[step], ahead.at[step, axis], target(axis, -1)))
            copies[-1].start()
        local = [None] * 8
        cols = [columns(phi[step, a:a + 1]) for a in range(8)]
        for axis in range(2):
            for a in range(8):
                back[step, axis, a:a + 1] = backward(blocks[a, 1 + axis], cols[a])
            copies.append(copy(step, 2 + axis, back.at[step, axis], got.at[step, axis], target(axis, 1)))
            copies[-1].start()
        sums = []
        rows = []
        for a in range(8):
            own = phi[step, a:a + 1]
            right = phi[step, (a + 1) % 8:(a + 1) % 8 + 1]
            re0, im0 = forward(blocks[a, 0] + blocks[a, 3], own)
            re1, im1 = forward(blocks[a, 4], right)
            sums.append((re0 + re1, im0 + im1))
            rows.append(backward(blocks[a, 3], cols[a]) + backward(blocks[(a + 7) % 8, 4], cols[(a + 7) % 8]))
        for item in copies:
            item.wait()
        for a in range(8):
            re, im = sums[a]
            for axis in range(2):
                more_re, more_im = forward(blocks[a, 1 + axis], ahead[step, axis, a:a + 1])
                re = re + more_re
                im = im + more_im
            re = jnp.sum(re, 1, keepdims=True)
            im = jnp.sum(im, 1, keepdims=True)
            total = jnp.sum(re * eye_re + im * eye_im, 0, keepdims=True) + rows[a]
            total = total + got[step, 0, a:a + 1] + got[step, 1, a:a + 1]
            if step == 0:
                phi[1, a:a + 1] = total
            else:
                out_ref[a:a + 1] = total


def shifted_2(value, axis, steps):
    count = lax.axis_size(axis)
    pairs = [(source, (source + steps) % count) for source in range(count)]
    return lax.ppermute(value, axis, pairs)


def per_device(null_vectors, gauge_links, coarse_in):
    vectors = null_vectors.reshape(2, 24, 4, 3, 16, 128).transpose(4, 2, 3, 0, 1, 5).reshape(16, 4, 3, 48, 128)
    links = gauge_links.reshape(72, 16, 128).transpose(1, 0, 2).astype(jnp.float32) * 0.5
    face_t = shifted_2(vectors[0:4], "ta", -1)
    face_z = shifted_2(vectors[0::4], "sa", -1)
    vmem = pl.BlockSpec(memory_space=pltpu.VMEM)
    limit = pltpu.CompilerParams(vmem_limit_bytes=48 * 1024 * 1024)
    plane_sums = pl.pallas_call(
        plane_kernel,
        out_shape=jax.ShapeDtypeStruct((2, 576, 240), jnp.float32),
        in_specs=[vmem] * 2,
        out_specs=vmem,
        scratch_shapes=[
            pltpu.VMEM((576, 128), jnp.bfloat16),
            pltpu.VMEM((2, 576, 1536), jnp.bfloat16),
            pltpu.VMEM((2, 240, 1536), jnp.bfloat16),
        ],
        compiler_params=limit,
        cost_estimate=pl.CostEstimate(flops=14_000_000_000, bytes_accessed=4_000_000, transcendentals=0),
    )(vectors, links)
    blocks = pl.pallas_call(
        line_kernel,
        out_shape=jax.ShapeDtypeStruct((8, 5, 48, 96), jnp.float32),
        in_specs=[vmem] * 5,
        out_specs=vmem,
        scratch_shapes=[
            pltpu.VMEM((192, 128), jnp.bfloat16),
            pltpu.VMEM((2, 192, 1536), jnp.bfloat16),
            pltpu.VMEM((2, 192, 1536), jnp.bfloat16),
            pltpu.VMEM((4, 2, 192, 192), jnp.float32),
            pltpu.VMEM((2, 4, 3, 48, 128), jnp.bfloat16),
        ],
        compiler_params=limit,
        cost_estimate=pl.CostEstimate(flops=6_000_000_000, bytes_accessed=6_000_000, transcendentals=0),
    )(vectors, links, face_t, face_z, plane_sums)
    rows = coarse_in.reshape(8, 96)
    out = pl.pallas_call(
        functools.partial(coarse_kernel, ("ta", "sa")),
        out_shape=jax.ShapeDtypeStruct((8, 96), jnp.float32),
        in_specs=[vmem] * 2,
        out_specs=vmem,
        scratch_shapes=[
            pltpu.VMEM((2, 8, 96), jnp.float32),
            pltpu.VMEM((2, 2, 8, 96), jnp.float32),
            pltpu.VMEM((2, 2, 8, 96), jnp.float32),
            pltpu.VMEM((2, 2, 8, 96), jnp.float32),
            pltpu.SemaphoreType.DMA((2, 4)),
            pltpu.SemaphoreType.DMA((2, 4)),
        ],
        compiler_params=pltpu.CompilerParams(
            collective_id=0, has_side_effects=True, vmem_limit_bytes=48 * 1024 * 1024),
    )(blocks, rows)
    stored = blocks.reshape(8, 5, 48, 2, 48).transpose(0, 1, 3, 2, 4).reshape(1, 1, 8, 5, 4608)
    return stored, out.reshape(1, 1, 8, 96)


def solution(mesh):
    placed = (
        P(None, None, None, None, "ta", "sa", None),
        P(None, None, None, None, "ta", "sa", None),
        P("ta", "sa", None, None),
    )
    return jax.shard_map(
        per_device,
        mesh=mesh,
        in_specs=placed,
        out_specs=(P("ta", "sa", None, None, None), P("ta", "sa", None, None)),
        check_vma=False,
    )
```

```python
import functools

import jax
import jax.numpy as jnp
from jax import lax
from jax.experimental import pallas as pl
from jax.experimental.pallas import tpu as pltpu
from jax.sharding import PartitionSpec as P

LAT_X = 32
MESH = pl.DeviceIdType.MESH

SOURCE = ((2, 3, 0, 1), (2, 3, 0, 1), (3, 2, 1, 0), (3, 2, 1, 0))
ODD_SIGN = (False, True, True, False)
PHASE = ((0, 0), (3, 1), (2, 0), (3, 1))


def turn(re, im, power):
    if power == 0:
        return re, im
    if power == 1:
        return -im, re
    if power == 2:
        return -re, -im
    return im, -re


def hop_rows(same, cross, chi):
    first, second = (same, cross) if chi == 0 else (cross, same)
    of_real = jnp.concatenate([first[0], second[0], first[1], second[1]], 0)
    of_imag = jnp.concatenate([first[1], second[1], -first[0], -second[0]], 0)
    return of_real.astype(jnp.bfloat16), of_imag.astype(jnp.bfloat16)


def place_hops(direction, slot, shifted, u_ref, a, h, right):
    links = []
    for q in range(2):
        links.append([[u_ref[a, h, pl.ds(((q * 4 + direction) * 3 + row) * 3 + col, 1), :]
                       for col in range(3)] for row in range(3)])
    for c in range(3):
        hops = []
        for s in range(4):
            re = None
            im = None
            for d in range(3):
                lr, li = links[0][c][d], links[1][c][d]
                vr, vi = shifted[s][d]
                term_r = lr * vr - li * vi
                term_i = lr * vi + li * vr
                re = term_r if re is None else re + term_r
                im = term_i if im is None else im + term_i
            hops.append((re, im))
        for s in range(4):
            chi = s // 2
            same = (-hops[s][0], -hops[s][1])
            power = PHASE[direction][chi]
            if ODD_SIGN[direction] and s % 2 == 1:
                power = (power + 2) % 4
            cross = turn(*hops[SOURCE[direction][s]], power)
            of_real, of_imag = hop_rows(same, cross, chi)
            k = (s % 2) * 3 + c
            right[chi, 96 * slot:96 * slot + 96, 128 * k:128 * k + 128] = of_real
            right[chi, 96 * slot:96 * slot + 96, 128 * (k + 6):128 * (k + 7)] = of_imag


def place_left(values, edges, left):
    for s in range(4):
        for c in range(3):
            for q in range(2):
                part = values[s][c][q]
                zero = jnp.zeros_like(part)
                rows = [part, jnp.where(edges[0], part, zero), jnp.where(edges[1], part, zero), zero]
                k = q * 6 + (s % 2) * 3 + c
                left[s // 2, :, 128 * k:128 * k + 128] = jnp.concatenate(rows, 0).astype(jnp.bfloat16)


def load(ref, *index):
    out = []
    for s in range(4):
        row = []
        for c in range(3):
            k = 48 * (s * 3 + c)
            whole = ref[*index, k:k + 48, :].astype(jnp.float32)
            row.append((whole[:24], whole[24:]))
        out.append(row)
    return out


def moved(move, *fields):
    return [[tuple(move(*(f[s][c][q] for f in fields)) for q in range(2)) for c in range(3)] for s in range(4)]


def product(left, right):
    return lax.dot_general(left, right, (((1,), (1,)), ((), ())), preferred_element_type=jnp.float32)


def spread_kernel(v_ref, u_ref, v_out, u_out, place):
    row = lax.broadcasted_iota(jnp.int32, (128, 1024), 0)
    col = lax.broadcasted_iota(jnp.int32, (128, 1024), 1)
    hit = row == col % 16 // 4 * LAT_X + col // 128 * 4 + col % 4
    for k in range(8):
        place[128 * k:128 * k + 128, :] = jnp.where(hit & (col % 128 // 16 == k), 1.0, 0.0).astype(jnp.bfloat16)
    for h in range(2):
        for ref, out in ((v_ref, v_out), (u_ref, u_out)):
            wide = jnp.concatenate([ref[8 * h + k] for k in range(8)], 1)
            found = jnp.dot(wide, place[...], preferred_element_type=jnp.float32)
            for a in range(8):
                part = found[:, 128 * a:128 * a + 128]
                out[a, h] = part.astype(jnp.bfloat16) if ref is v_ref else 0.5 * part


def plane_kernel(v_ref, u_ref, sums, left0, left1, right0, right1):
    lane = lax.broadcasted_iota(jnp.int32, (24, 128), 1)
    y_edge = lane // 4 % 4 == 3
    x_edge = lane % 4 == 3

    def ahead_y(part):
        return jnp.where(y_edge, pltpu.roll(part, 12, 1), pltpu.roll(part, 124, 1))

    def ahead_x(part, following):
        return jnp.where(x_edge, pltpu.roll(following, 3, 1), pltpu.roll(part, 127, 1))

    @pl.loop(0, 8)
    def _(a):
        after = lax.rem(a + 1, 8)
        for h, (left, right) in enumerate(((left0, right0), (left1, right1))):
            values = load(v_ref, a, h)
            place_left(values, (y_edge, x_edge), left)
            for s in range(4):
                for c in range(3):
                    vr, vi = values[s][c]
                    k = (s % 2) * 3 + c
                    right[s // 2, 192:240, 128 * k:128 * k + 128] = (
                        jnp.concatenate([vr, vi], 0).astype(jnp.bfloat16))
                    right[s // 2, 192:240, 128 * (k + 6):128 * (k + 7)] = (
                        jnp.concatenate([vi, -vr], 0).astype(jnp.bfloat16))
            place_hops(2, 0, moved(ahead_y, values), u_ref, a, h, right)
            place_hops(3, 1, moved(ahead_x, values, load(v_ref, after, h)), u_ref, a, h, right)
        for chi in range(2):
            sums[a, chi] = product(right0[chi], left0[chi]) + product(right1[chi], left1[chi])


def line_kernel(v_ref, u_ref, face_t, face_z, place, plane_sums, blocks, stored,
                far_t, far_z, left0, left1, right0, right1):
    wide = jnp.concatenate([face_t[k] for k in range(4)], 1)
    found = jnp.dot(wide, place[0:512, :], preferred_element_type=jnp.float32)
    for a in range(8):
        far_t[a] = found[:, 128 * a:128 * a + 128].astype(jnp.bfloat16)
    ends = jnp.concatenate([place[384:512, :], place[896:1024, :]], 0)
    for h in range(2):
        wide = jnp.concatenate([face_z[2 * h], face_z[2 * h + 1]], 1)
        found = jnp.dot(wide, ends, preferred_element_type=jnp.float32)
        for a in range(8):
            far_z[a, h] = found[:, 128 * a:128 * a + 128].astype(jnp.bfloat16)

    lane = lax.broadcasted_iota(jnp.int32, (24, 128), 1)
    upper = lane >= 64
    z_edge = lane // 16 % 4 == 3
    nowhere = lane < 0
    row = lax.broadcasted_iota(jnp.int32, (48, 48), 0)
    col = lax.broadcasted_iota(jnp.int32, (48, 48), 1)
    sign = jnp.where((row < 24) == (col < 24), 1.0, -1.0)
    zero = jnp.zeros((24, 24), jnp.float32)

    def ahead_t(part, following):
        return pltpu.roll(jnp.where(upper, part, following), 64, 1)

    def ahead_z(part, face):
        return jnp.where(z_edge, face, pltpu.roll(part, 112, 1))

    @pl.loop(0, 8)
    def _(a):
        for h, (left, right) in enumerate(((left0, right0), (left1, right1))):
            values = load(v_ref, a, h)
            place_left(values, (upper if h == 1 else nowhere, z_edge), left)
            following = load(v_ref, a, 1) if h == 0 else load(far_t, a)
            place_hops(0, 0, moved(ahead_t, values, following), u_ref, a, h, right)
            place_hops(1, 1, moved(ahead_z, values, load(far_z, a, h)), u_ref, a, h, right)
        line = []
        plane = []
        for chi in range(2):
            line.append(product(right0[chi], left0[chi]) + product(right1[chi], left1[chi]))
            plane.append(plane_sums[a, chi])

        def pick(sums, slot, kind):
            return jnp.concatenate(
                [part[96 * slot:96 * slot + 96, 24 * kind:24 * kind + 24] for part in sums], 1)

        inner = (pick(line, 0, 0) - pick(line, 0, 1)) + (pick(line, 1, 0) - pick(line, 1, 2))
        inner = inner + (pick(plane, 0, 0) - pick(plane, 0, 1)) + (pick(plane, 1, 0) - pick(plane, 1, 2))
        gram = []
        for part in range(2):
            rows = slice(192 + 24 * part, 216 + 24 * part)
            gram.append(jnp.concatenate([plane[0][rows, 0:24], zero], 1))
            gram.append(jnp.concatenate([zero, plane[1][rows, 0:24]], 1))
        whole = (inner + jnp.concatenate(gram, 0)).T
        whole = whole + jnp.concatenate([sign * inner[:48], -sign * inner[48:]], 1)
        kept = [whole, pick(line, 0, 1).T, pick(line, 1, 2).T, pick(plane, 0, 1).T, pick(plane, 1, 2).T]
        for i, block in enumerate(kept):
            blocks[a, i] = block
            stored[a, i, 0] = block[:, :48]
            stored[a, i, 1] = block[:, 48:]


def coarse_kernel(axes, blocks, phi_ref, out_ref, phi, ahead, back, got, send, recv):
    counts = [lax.axis_size(name) for name in axes]
    here = [lax.axis_index(name) for name in axes]

    def target(axis, step):
        spot = list(here)
        spot[axis] = lax.rem(here[axis] + step + counts[axis], counts[axis])
        return tuple(spot)

    barrier = pltpu.get_barrier_semaphore()
    for axis in range(2):
        for step in (-1, 1):
            pl.semaphore_signal(barrier, inc=1, device_id=target(axis, step), device_id_type=MESH)
    pl.semaphore_wait(barrier, 4)

    lane = lax.broadcasted_iota(jnp.int32, (1, 96), 1)
    row48 = lax.broadcasted_iota(jnp.int32, (48, 96), 0)
    lane48 = lax.broadcasted_iota(jnp.int32, (48, 96), 1)
    first = lane < 48
    gamma_row = jnp.where(lane % 48 < 24, 1.0, -1.0)
    gamma_col = jnp.where(lax.broadcasted_iota(jnp.int32, (48, 1), 0) < 24, 1.0, -1.0)
    eye_re = jnp.where(row48 == lane48, 1.0, 0.0)
    eye_im = jnp.where(row48 + 48 == lane48, 1.0, 0.0)

    def swapped(vector):
        return jnp.concatenate([vector[:, 48:], vector[:, :48]], 1)

    def forward(block, vector):
        other = swapped(vector)
        return block * jnp.where(first, vector, -vector), block * other

    def columns(vector):
        re = jnp.sum(vector * eye_re, 1, keepdims=True) * gamma_col
        im = jnp.sum(vector * eye_im, 1, keepdims=True) * gamma_col
        return re, im

    def backward(block, cols):
        re = jnp.sum(block * cols[0], 0, keepdims=True)
        im = jnp.sum(block * cols[1], 0, keepdims=True)
        other_im = swapped(im)
        return gamma_row * jnp.where(first, re + other_im, other_im - re)

    def copy(step, kind, src, dst, to):
        return pltpu.make_async_remote_copy(
            src_ref=src, dst_ref=dst, send_sem=send.at[step, kind], recv_sem=recv.at[step, kind],
            device_id=to, device_id_type=MESH)

    phi[0] = phi_ref[...]
    for step in range(2):
        copies = []
        for axis in range(2):
            copies.append(copy(step, axis, phi.at[step], ahead.at[step, axis], target(axis, -1)))
            copies[-1].start()
        local = [None] * 8
        cols = [columns(phi[step, a:a + 1]) for a in range(8)]
        for axis in range(2):
            for a in range(8):
                back[step, axis, a:a + 1] = backward(blocks[a, 1 + axis], cols[a])
            copies.append(copy(step, 2 + axis, back.at[step, axis], got.at[step, axis], target(axis, 1)))
            copies[-1].start()
        sums = []
        rows = []
        for a in range(8):
            own = phi[step, a:a + 1]
            right = phi[step, (a + 1) % 8:(a + 1) % 8 + 1]
            re0, im0 = forward(blocks[a, 0] + blocks[a, 3], own)
            re1, im1 = forward(blocks[a, 4], right)
            sums.append((re0 + re1, im0 + im1))
            rows.append(backward(blocks[a, 3], cols[a]) + backward(blocks[(a + 7) % 8, 4], cols[(a + 7) % 8]))
        for item in copies:
            item.wait()
        for a in range(8):
            re, im = sums[a]
            for axis in range(2):
                more_re, more_im = forward(blocks[a, 1 + axis], ahead[step, axis, a:a + 1])
                re = re + more_re
                im = im + more_im
            re = jnp.sum(re, 1, keepdims=True)
            im = jnp.sum(im, 1, keepdims=True)
            total = jnp.sum(re * eye_re + im * eye_im, 0, keepdims=True) + rows[a]
            total = total + got[step, 0, a:a + 1] + got[step, 1, a:a + 1]
            if step == 0:
                phi[1, a:a + 1] = total
            else:
                out_ref[a:a + 1] = total


def shifted_2(value, axis, steps):
    count = lax.axis_size(axis)
    pairs = [(source, (source + steps) % count) for source in range(count)]
    return lax.ppermute(value, axis, pairs)


def per_device(null_vectors, gauge_links, coarse_in):
    vectors = null_vectors.reshape(2, 24, 4, 3, 16, 128).transpose(4, 2, 3, 0, 1, 5).reshape(16, 576, 128)
    links = gauge_links.reshape(72, 16, 128).transpose(1, 0, 2)
    face_t = shifted_2(vectors[0:4], "ta", -1)
    face_z = shifted_2(vectors[0::4], "sa", -1)
    vmem = pl.BlockSpec(memory_space=pltpu.VMEM)
    limit = pltpu.CompilerParams(vmem_limit_bytes=48 * 1024 * 1024)
    spread_v, spread_u, place = pl.pallas_call(
        spread_kernel,
        out_shape=(
            jax.ShapeDtypeStruct((8, 2, 576, 128), jnp.bfloat16),
            jax.ShapeDtypeStruct((8, 2, 72, 128), jnp.float32),
            jax.ShapeDtypeStruct((1024, 1024), jnp.bfloat16),
        ),
        in_specs=[vmem] * 2,
        out_specs=(vmem, vmem, vmem),
        compiler_params=limit,
        cost_estimate=pl.CostEstimate(flops=2_700_000_000, bytes_accessed=7_000_000, transcendentals=0),
    )(vectors, links)
    operands = [
        pltpu.VMEM((2, 96, 1536), jnp.bfloat16),
        pltpu.VMEM((2, 96, 1536), jnp.bfloat16),
    ]
    plane_sums = pl.pallas_call(
        plane_kernel,
        out_shape=jax.ShapeDtypeStruct((8, 2, 240, 96), jnp.float32),
        in_specs=[vmem] * 2,
        out_specs=vmem,
        scratch_shapes=operands + [pltpu.VMEM((2, 240, 1536), jnp.bfloat16)] * 2,
        compiler_params=limit,
        cost_estimate=pl.CostEstimate(flops=8_000_000_000, bytes_accessed=4_000_000, transcendentals=0),
    )(spread_v, spread_u)
    blocks, stored = pl.pallas_call(
        line_kernel,
        out_shape=(
            jax.ShapeDtypeStruct((8, 5, 48, 96), jnp.float32),
            jax.ShapeDtypeStruct((8, 5, 2, 48, 48), jnp.float32),
        ),
        in_specs=[vmem] * 6,
        out_specs=(vmem, vmem),
        scratch_shapes=[
            pltpu.VMEM((8, 576, 128), jnp.bfloat16),
            pltpu.VMEM((8, 2, 576, 128), jnp.bfloat16),
        ] + operands + [pltpu.VMEM((2, 192, 1536), jnp.bfloat16)] * 2,
        compiler_params=limit,
        cost_estimate=pl.CostEstimate(flops=8_000_000_000, bytes_accessed=6_000_000, transcendentals=0),
    )(spread_v, spread_u, face_t, face_z, place, plane_sums)
    rows = coarse_in.reshape(8, 96)
    out = pl.pallas_call(
        functools.partial(coarse_kernel, ("ta", "sa")),
        out_shape=jax.ShapeDtypeStruct((8, 96), jnp.float32),
        in_specs=[vmem] * 2,
        out_specs=vmem,
        scratch_shapes=[
            pltpu.VMEM((2, 8, 96), jnp.float32),
            pltpu.VMEM((2, 2, 8, 96), jnp.float32),
            pltpu.VMEM((2, 2, 8, 96), jnp.float32),
            pltpu.VMEM((2, 2, 8, 96), jnp.float32),
            pltpu.SemaphoreType.DMA((2, 4)),
            pltpu.SemaphoreType.DMA((2, 4)),
        ],
        compiler_params=pltpu.CompilerParams(
            collective_id=0, has_side_effects=True, vmem_limit_bytes=48 * 1024 * 1024),
    )(blocks, rows)
    stored = stored.reshape(1, 1, 8, 5, 4608)
    return stored, out.reshape(1, 1, 8, 96)


def solution(mesh):
    placed = (
        P(None, None, None, None, "ta", "sa", None),
        P(None, None, None, None, "ta", "sa", None),
        P("ta", "sa", None, None),
    )
    return jax.shard_map(
        per_device,
        mesh=mesh,
        in_specs=placed,
        out_specs=(P("ta", "sa", None, None, None), P("ta", "sa", None, None)),
        check_vma=False,
    )
```

```python
import functools

import jax
import jax.numpy as jnp
from jax import lax
from jax.experimental import pallas as pl
from jax.experimental.pallas import tpu as pltpu
from jax.sharding import PartitionSpec as P

LAT_X = 32
MESH = pl.DeviceIdType.MESH

SOURCE = ((2, 3, 0, 1), (2, 3, 0, 1), (3, 2, 1, 0), (3, 2, 1, 0))
ODD_SIGN = (False, True, True, False)
PHASE = ((0, 0), (3, 1), (2, 0), (3, 1))


def turn(re, im, power):
    if power == 0:
        return re, im
    if power == 1:
        return -im, re
    if power == 2:
        return -re, -im
    return im, -re


def hop_rows(same, cross, chi):
    first, second = (same, cross) if chi == 0 else (cross, same)
    of_real = jnp.concatenate([first[0], second[0], first[1], second[1]], 0)
    of_imag = jnp.concatenate([first[1], second[1], -first[0], -second[0]], 0)
    return of_real.astype(jnp.bfloat16), of_imag.astype(jnp.bfloat16)


def place_hops(direction, slot, shifted, u_ref, a, h, right):
    sums = [[shifted[s][d][0] + shifted[s][d][1] for d in range(3)] for s in range(4)]
    for c in range(3):
        links = []
        for d in range(3):
            lr, li = [
                jnp.broadcast_to(u_ref[a, h, pl.ds(((q * 4 + direction) * 3 + c) * 3 + d, 1), :], (8, 128))
                for q in range(2)
            ]
            links.append((lr, li - lr, lr + li))
        hops = []
        for s in range(4):
            totals = None
            for d in range(3):
                factors = (sums[s][d], shifted[s][d][0], shifted[s][d][1])
                terms = [link[None] * f.reshape(3, 8, 128) for link, f in zip(links[d], factors)]
                totals = terms if totals is None else [x + y for x, y in zip(totals, terms)]
            hops.append(((totals[0] - totals[2]).reshape(24, 128), (totals[0] + totals[1]).reshape(24, 128)))
        for s in range(4):
            chi = s // 2
            same = (-hops[s][0], -hops[s][1])
            power = PHASE[direction][chi]
            if ODD_SIGN[direction] and s % 2 == 1:
                power = (power + 2) % 4
            cross = turn(*hops[SOURCE[direction][s]], power)
            of_real, of_imag = hop_rows(same, cross, chi)
            k = (s % 2) * 3 + c
            right[chi, 96 * slot:96 * slot + 96, 128 * k:128 * k + 128] = of_real
            right[chi, 96 * slot:96 * slot + 96, 128 * (k + 6):128 * (k + 7)] = of_imag


def place_left(values, edges, left):
    for s in range(4):
        for c in range(3):
            for q in range(2):
                part = values[s][c][q]
                zero = jnp.zeros_like(part)
                rows = [part, jnp.where(edges[0], part, zero), jnp.where(edges[1], part, zero), zero]
                k = q * 6 + (s % 2) * 3 + c
                left[s // 2, :, 128 * k:128 * k + 128] = jnp.concatenate(rows, 0).astype(jnp.bfloat16)


def load(ref, *index):
    out = []
    for s in range(4):
        row = []
        for c in range(3):
            k = 48 * (s * 3 + c)
            whole = ref[*index, k:k + 48, :].astype(jnp.float32)
            row.append((whole[:24], whole[24:]))
        out.append(row)
    return out


def moved(move, *fields):
    return [[tuple(move(*(f[s][c][q] for f in fields)) for q in range(2)) for c in range(3)] for s in range(4)]


def product(left, right):
    return lax.dot_general(left, right, (((1,), (1,)), ((), ())), preferred_element_type=jnp.float32)


def spread_kernel(v_ref, u_ref, v_out, u_out, place):
    row = lax.broadcasted_iota(jnp.int32, (128, 1024), 0)
    col = lax.broadcasted_iota(jnp.int32, (128, 1024), 1)
    hit = row == col % 16 // 4 * LAT_X + col // 128 * 4 + col % 4
    for k in range(8):
        place[128 * k:128 * k + 128, :] = jnp.where(hit & (col % 128 // 16 == k), 1.0, 0.0).astype(jnp.bfloat16)
    for h in range(2):
        for ref, out in ((v_ref, v_out), (u_ref, u_out)):
            wide = jnp.concatenate([ref[8 * h + k] for k in range(8)], 1)
            found = jnp.dot(wide, place[...], preferred_element_type=jnp.float32)
            for a in range(8):
                part = found[:, 128 * a:128 * a + 128]
                out[a, h] = part.astype(jnp.bfloat16) if ref is v_ref else 0.5 * part


def plane_kernel(v_ref, u_ref, sums, left0, left1, right0, right1):
    lane = lax.broadcasted_iota(jnp.int32, (24, 128), 1)
    y_edge = lane // 4 % 4 == 3
    x_edge = lane % 4 == 3

    def ahead_y(part):
        return jnp.where(y_edge, pltpu.roll(part, 12, 1), pltpu.roll(part, 124, 1))

    def ahead_x(part, following):
        return jnp.where(x_edge, pltpu.roll(following, 3, 1), pltpu.roll(part, 127, 1))

    @pl.loop(0, 8)
    def _(a):
        after = lax.rem(a + 1, 8)
        for h, (left, right) in enumerate(((left0, right0), (left1, right1))):
            values = load(v_ref, a, h)
            place_left(values, (y_edge, x_edge), left)
            for s in range(4):
                for c in range(3):
                    vr, vi = values[s][c]
                    k = (s % 2) * 3 + c
                    right[s // 2, 192:240, 128 * k:128 * k + 128] = (
                        jnp.concatenate([vr, vi], 0).astype(jnp.bfloat16))
                    right[s // 2, 192:240, 128 * (k + 6):128 * (k + 7)] = (
                        jnp.concatenate([vi, -vr], 0).astype(jnp.bfloat16))
            place_hops(2, 0, moved(ahead_y, values), u_ref, a, h, right)
            place_hops(3, 1, moved(ahead_x, values, load(v_ref, after, h)), u_ref, a, h, right)
        for chi in range(2):
            sums[a, chi] = product(right0[chi], left0[chi]) + product(right1[chi], left1[chi])


def line_kernel(v_ref, u_ref, face_t, face_z, place, plane_sums, blocks, stored,
                far_t, far_z, flat, left0, left1, right0, right1):
    wide = jnp.concatenate([face_t[k] for k in range(4)], 1)
    found = jnp.dot(wide, place[0:512, :], preferred_element_type=jnp.float32)
    for a in range(8):
        far_t[a] = found[:, 128 * a:128 * a + 128].astype(jnp.bfloat16)
    ends = jnp.concatenate([place[384:512, :], place[896:1024, :]], 0)
    for h in range(2):
        wide = jnp.concatenate([face_z[2 * h], face_z[2 * h + 1]], 1)
        found = jnp.dot(wide, ends, preferred_element_type=jnp.float32)
        for a in range(8):
            far_z[a, h] = found[:, 128 * a:128 * a + 128].astype(jnp.bfloat16)

    lane = lax.broadcasted_iota(jnp.int32, (24, 128), 1)
    upper = lane >= 64
    z_edge = lane // 16 % 4 == 3
    nowhere = lane < 0
    row = lax.broadcasted_iota(jnp.int32, (48, 48), 0)
    col = lax.broadcasted_iota(jnp.int32, (48, 48), 1)
    sign = jnp.where((row < 24) == (col < 24), 1.0, -1.0)
    zero = jnp.zeros((24, 24), jnp.float32)

    def ahead_t(part, following):
        return pltpu.roll(jnp.where(upper, part, following), 64, 1)

    def ahead_z(part, face):
        return jnp.where(z_edge, face, pltpu.roll(part, 112, 1))

    @pl.loop(0, 8)
    def _(a):
        for h, (left, right) in enumerate(((left0, right0), (left1, right1))):
            values = load(v_ref, a, h)
            place_left(values, (upper if h == 1 else nowhere, z_edge), left)
            following = load(v_ref, a, 1) if h == 0 else load(far_t, a)
            place_hops(0, 0, moved(ahead_t, values, following), u_ref, a, h, right)
            place_hops(1, 1, moved(ahead_z, values, load(far_z, a, h)), u_ref, a, h, right)
        line = []
        plane = []
        for chi in range(2):
            line.append(product(right0[chi], left0[chi]) + product(right1[chi], left1[chi]))
            plane.append(plane_sums[a, chi])

        def pick(sums, slot, kind):
            return jnp.concatenate(
                [part[96 * slot:96 * slot + 96, 24 * kind:24 * kind + 24] for part in sums], 1)

        inner = (pick(line, 0, 0) - pick(line, 0, 1)) + (pick(line, 1, 0) - pick(line, 1, 2))
        inner = inner + (pick(plane, 0, 0) - pick(plane, 0, 1)) + (pick(plane, 1, 0) - pick(plane, 1, 2))
        gram = []
        for part in range(2):
            rows = slice(192 + 24 * part, 216 + 24 * part)
            gram.append(jnp.concatenate([plane[0][rows, 0:24], zero], 1))
            gram.append(jnp.concatenate([zero, plane[1][rows, 0:24]], 1))
        whole = (inner + jnp.concatenate(gram, 0)).T
        whole = whole + jnp.concatenate([sign * inner[:48], -sign * inner[48:]], 1)
        kept = [whole, pick(line, 0, 1).T, pick(line, 1, 2).T, pick(plane, 0, 1).T, pick(plane, 1, 2).T]
        for i, block in enumerate(kept):
            blocks[a, i] = block
            flat[pl.ds(pl.multiple_of(a * 240 + i * 48, 8), 48), 0:96] = block

    for i in range(5):
        for g in range(6):
            group = [flat[pl.ds(i * 48 + g * 8 + v, 8, stride=240), :] for v in range(8)]
            stored[i, :, 384 * g:384 * g + 384] = jnp.concatenate([x[:, :48] for x in group], 1)
            stored[i, :, 2304 + 384 * g:2688 + 384 * g] = jnp.concatenate([x[:, 48:96] for x in group], 1)


def coarse_kernel(axes, blocks, phi_ref, out_ref, phi, ahead, back, got, send, recv):
    counts = [lax.axis_size(name) for name in axes]
    here = [lax.axis_index(name) for name in axes]

    def target(axis, step):
        spot = list(here)
        spot[axis] = lax.rem(here[axis] + step + counts[axis], counts[axis])
        return tuple(spot)

    barrier = pltpu.get_barrier_semaphore()
    for axis in range(2):
        for step in (-1, 1):
            pl.semaphore_signal(barrier, inc=1, device_id=target(axis, step), device_id_type=MESH)
    pl.semaphore_wait(barrier, 4)

    lane = lax.broadcasted_iota(jnp.int32, (1, 96), 1)
    row48 = lax.broadcasted_iota(jnp.int32, (48, 96), 0)
    lane48 = lax.broadcasted_iota(jnp.int32, (48, 96), 1)
    first = lane < 48
    gamma_row = jnp.where(lane % 48 < 24, 1.0, -1.0)
    gamma_col = jnp.where(lax.broadcasted_iota(jnp.int32, (48, 1), 0) < 24, 1.0, -1.0)
    eye_re = jnp.where(row48 == lane48, 1.0, 0.0)
    eye_im = jnp.where(row48 + 48 == lane48, 1.0, 0.0)

    def swapped(vector):
        return jnp.concatenate([vector[:, 48:], vector[:, :48]], 1)

    def forward(block, vector):
        other = swapped(vector)
        return block * jnp.where(first, vector, -vector), block * other

    def columns(vector):
        re = jnp.sum(vector * eye_re, 1, keepdims=True) * gamma_col
        im = jnp.sum(vector * eye_im, 1, keepdims=True) * gamma_col
        return re, im

    def backward(block, cols):
        re = jnp.sum(block * cols[0], 0, keepdims=True)
        im = jnp.sum(block * cols[1], 0, keepdims=True)
        other_im = swapped(im)
        return gamma_row * jnp.where(first, re + other_im, other_im - re)

    def copy(step, kind, src, dst, to):
        return pltpu.make_async_remote_copy(
            src_ref=src, dst_ref=dst, send_sem=send.at[step, kind], recv_sem=recv.at[step, kind],
            device_id=to, device_id_type=MESH)

    phi[0] = phi_ref[...]
    for step in range(2):
        copies = []
        for axis in range(2):
            copies.append(copy(step, axis, phi.at[step], ahead.at[step, axis], target(axis, -1)))
            copies[-1].start()
        local = [None] * 8
        cols = [columns(phi[step, a:a + 1]) for a in range(8)]
        for axis in range(2):
            for a in range(8):
                back[step, axis, a:a + 1] = backward(blocks[a, 1 + axis], cols[a])
            copies.append(copy(step, 2 + axis, back.at[step, axis], got.at[step, axis], target(axis, 1)))
            copies[-1].start()
        sums = []
        rows = []
        for a in range(8):
            own = phi[step, a:a + 1]
            right = phi[step, (a + 1) % 8:(a + 1) % 8 + 1]
            re0, im0 = forward(blocks[a, 0] + blocks[a, 3], own)
            re1, im1 = forward(blocks[a, 4], right)
            sums.append((re0 + re1, im0 + im1))
            rows.append(backward(blocks[a, 3], cols[a]) + backward(blocks[(a + 7) % 8, 4], cols[(a + 7) % 8]))
        for item in copies:
            item.wait()
        for a in range(8):
            re, im = sums[a]
            for axis in range(2):
                more_re, more_im = forward(blocks[a, 1 + axis], ahead[step, axis, a:a + 1])
                re = re + more_re
                im = im + more_im
            re = jnp.sum(re, 1, keepdims=True)
            im = jnp.sum(im, 1, keepdims=True)
            total = jnp.sum(re * eye_re + im * eye_im, 0, keepdims=True) + rows[a]
            total = total + got[step, 0, a:a + 1] + got[step, 1, a:a + 1]
            if step == 0:
                phi[1, a:a + 1] = total
            else:
                out_ref[a:a + 1] = total


def shifted_2(value, axis, steps):
    count = lax.axis_size(axis)
    pairs = [(source, (source + steps) % count) for source in range(count)]
    return lax.ppermute(value, axis, pairs)


def per_device(null_vectors, gauge_links, coarse_in):
    vectors = null_vectors.reshape(2, 24, 4, 3, 16, 128).transpose(4, 2, 3, 0, 1, 5).reshape(16, 576, 128)
    links = gauge_links.reshape(72, 16, 128).transpose(1, 0, 2)
    face_t = shifted_2(vectors[0:4], "ta", -1)
    face_z = shifted_2(vectors[0::4], "sa", -1)
    vmem = pl.BlockSpec(memory_space=pltpu.VMEM)
    limit = pltpu.CompilerParams(vmem_limit_bytes=24 * 1024 * 1024)
    spread_v, spread_u, place = pl.pallas_call(
        spread_kernel,
        out_shape=(
            jax.ShapeDtypeStruct((8, 2, 576, 128), jnp.bfloat16),
            jax.ShapeDtypeStruct((8, 2, 72, 128), jnp.float32),
            jax.ShapeDtypeStruct((1024, 1024), jnp.bfloat16),
        ),
        in_specs=[vmem] * 2,
        out_specs=(vmem, vmem, vmem),
        compiler_params=limit,
        cost_estimate=pl.CostEstimate(flops=2_700_000_000, bytes_accessed=7_000_000, transcendentals=0),
    )(vectors, links)
    operands = [
        pltpu.VMEM((2, 96, 1536), jnp.bfloat16),
        pltpu.VMEM((2, 96, 1536), jnp.bfloat16),
    ]
    plane_sums = pl.pallas_call(
        plane_kernel,
        out_shape=jax.ShapeDtypeStruct((8, 2, 240, 96), jnp.float32),
        in_specs=[vmem] * 2,
        out_specs=vmem,
        scratch_shapes=operands + [pltpu.VMEM((2, 240, 1536), jnp.bfloat16)] * 2,
        compiler_params=limit,
        cost_estimate=pl.CostEstimate(flops=8_000_000_000, bytes_accessed=4_000_000, transcendentals=0),
    )(spread_v, spread_u)
    blocks, stored = pl.pallas_call(
        line_kernel,
        out_shape=(
            jax.ShapeDtypeStruct((8, 5, 48, 96), jnp.float32),
            jax.ShapeDtypeStruct((5, 8, 4608), jnp.float32),
        ),
        in_specs=[vmem] * 6,
        out_specs=(vmem, vmem),
        scratch_shapes=[
            pltpu.VMEM((8, 576, 128), jnp.bfloat16),
            pltpu.VMEM((8, 2, 576, 128), jnp.bfloat16),
            pltpu.VMEM((1920, 128), jnp.float32),
        ] + operands + [pltpu.VMEM((2, 192, 1536), jnp.bfloat16)] * 2,
        compiler_params=limit,
        cost_estimate=pl.CostEstimate(flops=8_000_000_000, bytes_accessed=6_000_000, transcendentals=0),
    )(spread_v, spread_u, face_t, face_z, place, plane_sums)
    rows = coarse_in.reshape(8, 96)
    out = pl.pallas_call(
        functools.partial(coarse_kernel, ("ta", "sa")),
        out_shape=jax.ShapeDtypeStruct((8, 96), jnp.float32),
        in_specs=[vmem] * 2,
        out_specs=vmem,
        scratch_shapes=[
            pltpu.VMEM((2, 8, 96), jnp.float32),
            pltpu.VMEM((2, 2, 8, 96), jnp.float32),
            pltpu.VMEM((2, 2, 8, 96), jnp.float32),
            pltpu.VMEM((2, 2, 8, 96), jnp.float32),
            pltpu.SemaphoreType.DMA((2, 4)),
            pltpu.SemaphoreType.DMA((2, 4)),
        ],
        compiler_params=pltpu.CompilerParams(
            collective_id=0, has_side_effects=True, vmem_limit_bytes=16 * 1024 * 1024),
    )(blocks, rows)
    stored = stored.transpose(1, 0, 2).reshape(1, 1, 8, 5, 4608)
    return stored, out.reshape(1, 1, 8, 96)


def solution(mesh):
    placed = (
        P(None, None, None, None, "ta", "sa", None),
        P(None, None, None, None, "ta", "sa", None),
        P("ta", "sa", None, None),
    )
    return jax.shard_map(
        per_device,
        mesh=mesh,
        in_specs=placed,
        out_specs=(P("ta", "sa", None, None, None), P("ta", "sa", None, None)),
        check_vma=False,
    )
```

```python
import functools

import jax
import jax.numpy as jnp
from jax import lax
from jax.experimental import pallas as pl
from jax.experimental.pallas import tpu as pltpu
from jax.sharding import PartitionSpec as P

LAT_X = 32
MESH = pl.DeviceIdType.MESH

SOURCE = ((2, 3, 0, 1), (2, 3, 0, 1), (3, 2, 1, 0), (3, 2, 1, 0))
ODD_SIGN = (False, True, True, False)
PHASE = ((0, 0), (3, 1), (2, 0), (3, 1))


def turn(re, im, power):
    if power == 0:
        return re, im
    if power == 1:
        return -im, re
    if power == 2:
        return -re, -im
    return im, -re


def place_hops(directions, shifted, u_ref, a, h, flip, right):
    sums = [[[f[s][d][0] + f[s][d][1] for d in range(3)] for s in range(4)] for f in shifted]
    for c in range(3):
        hops = []
        for slot, direction in enumerate(directions):
            links = []
            for d in range(3):
                lr, li = [
                    jnp.broadcast_to(u_ref[a, h, pl.ds(((q * 4 + direction) * 3 + c) * 3 + d, 1), :], (8, 128))
                    for q in range(2)
                ]
                links.append((lr, li - lr, lr + li))
            of_spin = []
            for s in range(4):
                totals = None
                for d in range(3):
                    factors = (sums[slot][s][d], shifted[slot][s][d][0], shifted[slot][s][d][1])
                    terms = [link[None] * f.reshape(3, 8, 128) for link, f in zip(links[d], factors)]
                    totals = terms if totals is None else [x + y for x, y in zip(totals, terms)]
                of_spin.append(((totals[0] - totals[2]).reshape(24, 128), (totals[0] + totals[1]).reshape(24, 128)))
            hops.append(of_spin)
        for s in range(4):
            other = SOURCE[directions[0]][s]
            k = (s % 2) * 3 + c
            k_cross = (other % 2) * 3 + c
            for q in range(2):
                both = jnp.concatenate([hops[0][s][q], hops[1][s][q]], 0).astype(jnp.bfloat16)
                right[s // 2, 48 * q:48 * q + 48, 128 * k:128 * k + 128] = both
                if other % 2 == 1:
                    both = both * flip
                right[other // 2, 96 + 48 * q:144 + 48 * q, 128 * k_cross:128 * k_cross + 128] = both


def place_left(values, edges, left):
    for s in range(4):
        for c in range(3):
            rows = []
            for part in values[s][c]:
                zero = jnp.zeros_like(part)
                rows += [part, jnp.where(edges[0], part, zero), jnp.where(edges[1], part, zero)]
            k = (s % 2) * 3 + c
            left[s // 2, :, 128 * k:128 * k + 128] = jnp.concatenate(rows, 0).astype(jnp.bfloat16)


def joined(of_re, of_im):
    return of_re[:, :72] + of_im[:, 72:], of_im[:, :72] - of_re[:, 72:]


def combine(raw, directions, chi):
    same = joined(raw[0:48], raw[48:96])
    cross = joined(raw[96:144], raw[144:192])
    rows = []
    for slot, direction in enumerate(directions):
        span = slice(24 * slot, 24 * slot + 24)
        pair = [(-same[0][span], -same[1][span]), turn(cross[0][span], cross[1][span], PHASE[direction][chi])]
        first, second = pair if chi == 0 else pair[::-1]
        rows += [first[0], second[0], first[1], second[1]]
    if raw.shape[0] == 240:
        rows += joined(raw[192:216], raw[216:240])
    return jnp.concatenate(rows, 0)


def flips(odd_slot):
    row = lax.broadcasted_iota(jnp.int32, (48, 128), 0)
    return jnp.where(row // 24 == odd_slot, -1.0, 1.0).astype(jnp.bfloat16)


def load(ref, *index):
    out = []
    for s in range(4):
        row = []
        for c in range(3):
            k = 48 * (s * 3 + c)
            whole = ref[*index, k:k + 48, :].astype(jnp.float32)
            row.append((whole[:24], whole[24:]))
        out.append(row)
    return out


def moved(move, *fields):
    return [[tuple(move(*(f[s][c][q] for f in fields)) for q in range(2)) for c in range(3)] for s in range(4)]


def product(left, right):
    return lax.dot_general(left, right, (((1,), (1,)), ((), ())), preferred_element_type=jnp.float32)


def spread_kernel(v_ref, u_ref, v_out, u_out, place):
    row = lax.broadcasted_iota(jnp.int32, (128, 1024), 0)
    col = lax.broadcasted_iota(jnp.int32, (128, 1024), 1)
    hit = row == col % 16 // 4 * LAT_X + col // 128 * 4 + col % 4
    for k in range(8):
        place[128 * k:128 * k + 128, :] = jnp.where(hit & (col % 128 // 16 == k), 1.0, 0.0).astype(jnp.bfloat16)
    for h in range(2):
        for ref, out in ((v_ref, v_out), (u_ref, u_out)):
            wide = jnp.concatenate([ref[8 * h + k] for k in range(8)], 1)
            found = jnp.dot(wide, place[...], preferred_element_type=jnp.float32)
            for a in range(8):
                part = found[:, 128 * a:128 * a + 128]
                out[a, h] = part.astype(jnp.bfloat16) if ref is v_ref else 0.5 * part


def plane_kernel(v_ref, u_ref, sums, left0, left1, right0, right1):
    lane = lax.broadcasted_iota(jnp.int32, (24, 128), 1)
    flip = flips(0)
    y_edge = lane // 4 % 4 == 3
    x_edge = lane % 4 == 3

    def ahead_y(part):
        return jnp.where(y_edge, pltpu.roll(part, 12, 1), pltpu.roll(part, 124, 1))

    def ahead_x(part, following):
        return jnp.where(x_edge, pltpu.roll(following, 3, 1), pltpu.roll(part, 127, 1))

    @pl.loop(0, 8)
    def _(a):
        after = lax.rem(a + 1, 8)
        for h, (left, right) in enumerate(((left0, right0), (left1, right1))):
            values = load(v_ref, a, h)
            place_left(values, (y_edge, x_edge), left)
            for s in range(4):
                for c in range(3):
                    vr, vi = values[s][c]
                    k = (s % 2) * 3 + c
                    right[s // 2, 192:240, 128 * k:128 * k + 128] = (
                        jnp.concatenate([vr, vi], 0).astype(jnp.bfloat16))
            ahead = (moved(ahead_y, values), moved(ahead_x, values, load(v_ref, after, h)))
            place_hops((2, 3), ahead, u_ref, a, h, flip, right)
        for chi in range(2):
            raw = product(right0[chi], left0[chi]) + product(right1[chi], left1[chi])
            sums[a, chi] = combine(raw, (2, 3), chi)


def line_kernel(v_ref, u_ref, face_t, face_z, place, plane_sums, blocks, stored,
                far_t, far_z, flat, left0, left1, right0, right1):
    wide = jnp.concatenate([face_t[k] for k in range(4)], 1)
    found = jnp.dot(wide, place[0:512, :], preferred_element_type=jnp.float32)
    for a in range(8):
        far_t[a] = found[:, 128 * a:128 * a + 128].astype(jnp.bfloat16)
    ends = jnp.concatenate([place[384:512, :], place[896:1024, :]], 0)
    for h in range(2):
        wide = jnp.concatenate([face_z[2 * h], face_z[2 * h + 1]], 1)
        found = jnp.dot(wide, ends, preferred_element_type=jnp.float32)
        for a in range(8):
            far_z[a, h] = found[:, 128 * a:128 * a + 128].astype(jnp.bfloat16)

    lane = lax.broadcasted_iota(jnp.int32, (24, 128), 1)
    flip = flips(1)
    upper = lane >= 64
    z_edge = lane // 16 % 4 == 3
    nowhere = lane < 0
    row = lax.broadcasted_iota(jnp.int32, (48, 48), 0)
    col = lax.broadcasted_iota(jnp.int32, (48, 48), 1)
    sign = jnp.where((row < 24) == (col < 24), 1.0, -1.0)
    zero = jnp.zeros((24, 24), jnp.float32)

    def ahead_t(part, following):
        return pltpu.roll(jnp.where(upper, part, following), 64, 1)

    def ahead_z(part, face):
        return jnp.where(z_edge, face, pltpu.roll(part, 112, 1))

    @pl.loop(0, 8)
    def _(a):
        for h, (left, right) in enumerate(((left0, right0), (left1, right1))):
            values = load(v_ref, a, h)
            place_left(values, (upper if h == 1 else nowhere, z_edge), left)
            following = load(v_ref, a, 1) if h == 0 else load(far_t, a)
            ahead = (moved(ahead_t, values, following), moved(ahead_z, values, load(far_z, a, h)))
            place_hops((0, 1), ahead, u_ref, a, h, flip, right)
        line = []
        plane = []
        for chi in range(2):
            raw = product(right0[chi], left0[chi]) + product(right1[chi], left1[chi])
            line.append(combine(raw, (0, 1), chi))
            plane.append(plane_sums[a, chi])

        def pick(sums, slot, kind):
            return jnp.concatenate(
                [part[96 * slot:96 * slot + 96, 24 * kind:24 * kind + 24] for part in sums], 1)

        inner = (pick(line, 0, 0) - pick(line, 0, 1)) + (pick(line, 1, 0) - pick(line, 1, 2))
        inner = inner + (pick(plane, 0, 0) - pick(plane, 0, 1)) + (pick(plane, 1, 0) - pick(plane, 1, 2))
        gram = []
        for part in range(2):
            rows = slice(192 + 24 * part, 216 + 24 * part)
            gram.append(jnp.concatenate([plane[0][rows, 0:24], zero], 1))
            gram.append(jnp.concatenate([zero, plane[1][rows, 0:24]], 1))
        whole = (inner + jnp.concatenate(gram, 0)).T
        whole = whole + jnp.concatenate([sign * inner[:48], -sign * inner[48:]], 1)
        kept = [whole, pick(line, 0, 1).T, pick(line, 1, 2).T, pick(plane, 0, 1).T, pick(plane, 1, 2).T]
        for i, block in enumerate(kept):
            blocks[a, i] = block
            flat[pl.ds(pl.multiple_of(a * 240 + i * 48, 8), 48), 0:96] = block

    for i in range(5):
        for g in range(6):
            group = [flat[pl.ds(i * 48 + g * 8 + v, 8, stride=240), :] for v in range(8)]
            stored[i, :, 384 * g:384 * g + 384] = jnp.concatenate([x[:, :48] for x in group], 1)
            stored[i, :, 2304 + 384 * g:2688 + 384 * g] = jnp.concatenate([x[:, 48:96] for x in group], 1)


def coarse_kernel(axes, blocks, phi_ref, out_ref, phi, ahead, back, got, send, recv):
    counts = [lax.axis_size(name) for name in axes]
    here = [lax.axis_index(name) for name in axes]

    def target(axis, step):
        spot = list(here)
        spot[axis] = lax.rem(here[axis] + step + counts[axis], counts[axis])
        return tuple(spot)

    barrier = pltpu.get_barrier_semaphore()
    for axis in range(2):
        for step in (-1, 1):
            pl.semaphore_signal(barrier, inc=1, device_id=target(axis, step), device_id_type=MESH)
    pl.semaphore_wait(barrier, 4)

    lane = lax.broadcasted_iota(jnp.int32, (1, 96), 1)
    row48 = lax.broadcasted_iota(jnp.int32, (48, 96), 0)
    lane48 = lax.broadcasted_iota(jnp.int32, (48, 96), 1)
    first = lane < 48
    gamma_row = jnp.where(lane % 48 < 24, 1.0, -1.0)
    gamma_col = jnp.where(lax.broadcasted_iota(jnp.int32, (48, 1), 0) < 24, 1.0, -1.0)
    eye_re = jnp.where(row48 == lane48, 1.0, 0.0)
    eye_im = jnp.where(row48 + 48 == lane48, 1.0, 0.0)

    def swapped(vector):
        return jnp.concatenate([vector[:, 48:], vector[:, :48]], 1)

    def forward(block, vector):
        other = swapped(vector)
        return block * jnp.where(first, vector, -vector), block * other

    def columns(vector):
        re = jnp.sum(vector * eye_re, 1, keepdims=True) * gamma_col
        im = jnp.sum(vector * eye_im, 1, keepdims=True) * gamma_col
        return re, im

    def backward(block, cols):
        re = jnp.sum(block * cols[0], 0, keepdims=True)
        im = jnp.sum(block * cols[1], 0, keepdims=True)
        other_im = swapped(im)
        return gamma_row * jnp.where(first, re + other_im, other_im - re)

    def copy(step, kind, src, dst, to):
        return pltpu.make_async_remote_copy(
            src_ref=src, dst_ref=dst, send_sem=send.at[step, kind], recv_sem=recv.at[step, kind],
            device_id=to, device_id_type=MESH)

    phi[0] = phi_ref[...]
    for step in range(2):
        copies = []
        for axis in range(2):
            copies.append(copy(step, axis, phi.at[step], ahead.at[step, axis], target(axis, -1)))
            copies[-1].start()
        local = [None] * 8
        cols = [columns(phi[step, a:a + 1]) for a in range(8)]
        for axis in range(2):
            for a in range(8):
                back[step, axis, a:a + 1] = backward(blocks[a, 1 + axis], cols[a])
            copies.append(copy(step, 2 + axis, back.at[step, axis], got.at[step, axis], target(axis, 1)))
            copies[-1].start()
        sums = []
        rows = []
        for a in range(8):
            own = phi[step, a:a + 1]
            right = phi[step, (a + 1) % 8:(a + 1) % 8 + 1]
            re0, im0 = forward(blocks[a, 0] + blocks[a, 3], own)
            re1, im1 = forward(blocks[a, 4], right)
            sums.append((re0 + re1, im0 + im1))
            rows.append(backward(blocks[a, 3], cols[a]) + backward(blocks[(a + 7) % 8, 4], cols[(a + 7) % 8]))
        for item in copies:
            item.wait()
        for a in range(8):
            re, im = sums[a]
            for axis in range(2):
                more_re, more_im = forward(blocks[a, 1 + axis], ahead[step, axis, a:a + 1])
                re = re + more_re
                im = im + more_im
            re = jnp.sum(re, 1, keepdims=True)
            im = jnp.sum(im, 1, keepdims=True)
            total = jnp.sum(re * eye_re + im * eye_im, 0, keepdims=True) + rows[a]
            total = total + got[step, 0, a:a + 1] + got[step, 1, a:a + 1]
            if step == 0:
                phi[1, a:a + 1] = total
            else:
                out_ref[a:a + 1] = total


def shifted_2(value, axis, steps):
    count = lax.axis_size(axis)
    pairs = [(source, (source + steps) % count) for source in range(count)]
    return lax.ppermute(value, axis, pairs)


def per_device(null_vectors, gauge_links, coarse_in):
    vectors = null_vectors.reshape(2, 24, 4, 3, 16, 128).transpose(4, 2, 3, 0, 1, 5).reshape(16, 576, 128)
    links = gauge_links.reshape(72, 16, 128).transpose(1, 0, 2)
    face_t = shifted_2(vectors[0:4], "ta", -1)
    face_z = shifted_2(vectors[0::4], "sa", -1)
    vmem = pl.BlockSpec(memory_space=pltpu.VMEM)
    limit = pltpu.CompilerParams(vmem_limit_bytes=24 * 1024 * 1024)
    spread_v, spread_u, place = pl.pallas_call(
        spread_kernel,
        out_shape=(
            jax.ShapeDtypeStruct((8, 2, 576, 128), jnp.bfloat16),
            jax.ShapeDtypeStruct((8, 2, 72, 128), jnp.float32),
            jax.ShapeDtypeStruct((1024, 1024), jnp.bfloat16),
        ),
        in_specs=[vmem] * 2,
        out_specs=(vmem, vmem, vmem),
        compiler_params=limit,
        cost_estimate=pl.CostEstimate(flops=2_700_000_000, bytes_accessed=7_000_000, transcendentals=0),
    )(vectors, links)
    operands = [
        pltpu.VMEM((2, 144, 768), jnp.bfloat16),
        pltpu.VMEM((2, 144, 768), jnp.bfloat16),
    ]
    plane_sums = pl.pallas_call(
        plane_kernel,
        out_shape=jax.ShapeDtypeStruct((8, 2, 240, 72), jnp.float32),
        in_specs=[vmem] * 2,
        out_specs=vmem,
        scratch_shapes=operands + [pltpu.VMEM((2, 240, 768), jnp.bfloat16)] * 2,
        compiler_params=limit,
        cost_estimate=pl.CostEstimate(flops=8_000_000_000, bytes_accessed=4_000_000, transcendentals=0),
    )(spread_v, spread_u)
    blocks, stored = pl.pallas_call(
        line_kernel,
        out_shape=(
            jax.ShapeDtypeStruct((8, 5, 48, 96), jnp.float32),
            jax.ShapeDtypeStruct((5, 8, 4608), jnp.float32),
        ),
        in_specs=[vmem] * 6,
        out_specs=(vmem, vmem),
        scratch_shapes=[
            pltpu.VMEM((8, 576, 128), jnp.bfloat16),
            pltpu.VMEM((8, 2, 576, 128), jnp.bfloat16),
            pltpu.VMEM((1920, 128), jnp.float32),
        ] + operands + [pltpu.VMEM((2, 192, 768), jnp.bfloat16)] * 2,
        compiler_params=limit,
        cost_estimate=pl.CostEstimate(flops=8_000_000_000, bytes_accessed=6_000_000, transcendentals=0),
    )(spread_v, spread_u, face_t, face_z, place, plane_sums)
    rows = coarse_in.reshape(8, 96)
    out = pl.pallas_call(
        functools.partial(coarse_kernel, ("ta", "sa")),
        out_shape=jax.ShapeDtypeStruct((8, 96), jnp.float32),
        in_specs=[vmem] * 2,
        out_specs=vmem,
        scratch_shapes=[
            pltpu.VMEM((2, 8, 96), jnp.float32),
            pltpu.VMEM((2, 2, 8, 96), jnp.float32),
            pltpu.VMEM((2, 2, 8, 96), jnp.float32),
            pltpu.VMEM((2, 2, 8, 96), jnp.float32),
            pltpu.SemaphoreType.DMA((2, 4)),
            pltpu.SemaphoreType.DMA((2, 4)),
        ],
        compiler_params=pltpu.CompilerParams(
            collective_id=0, has_side_effects=True, vmem_limit_bytes=16 * 1024 * 1024),
    )(blocks, rows)
    stored = stored.transpose(1, 0, 2).reshape(1, 1, 8, 5, 4608)
    return stored, out.reshape(1, 1, 8, 96)


def solution(mesh):
    placed = (
        P(None, None, None, None, "ta", "sa", None),
        P(None, None, None, None, "ta", "sa", None),
        P("ta", "sa", None, None),
    )
    return jax.shard_map(
        per_device,
        mesh=mesh,
        in_specs=placed,
        out_specs=(P("ta", "sa", None, None, None), P("ta", "sa", None, None)),
        check_vma=False,
    )
```

```python
import functools

import jax
import jax.numpy as jnp
from jax import lax
from jax.experimental import pallas as pl
from jax.experimental.pallas import tpu as pltpu
from jax.sharding import PartitionSpec as P

LAT_X = 32
MESH = pl.DeviceIdType.MESH

SOURCE = ((2, 3, 0, 1), (2, 3, 0, 1), (3, 2, 1, 0), (3, 2, 1, 0))
PHASE = ((0, 0), (3, 1), (2, 0), (3, 1))


def turn(re, im, power):
    if power == 0:
        return re, im
    if power == 1:
        return -im, re
    if power == 2:
        return -re, -im
    return im, -re


def place_hops(directions, shifted, u_ref, a, h, flip, right):
    sums = [[[f[s][d][0] + f[s][d][1] for d in range(3)] for s in range(4)] for f in shifted]
    for c in range(3):
        hops = []
        for slot, direction in enumerate(directions):
            links = []
            for d in range(3):
                lr, li = [
                    jnp.broadcast_to(u_ref[a, h, pl.ds(((q * 4 + direction) * 3 + c) * 3 + d, 1), :], (8, 128))
                    for q in range(2)
                ]
                links.append((lr, li - lr, lr + li))
            of_spin = []
            for s in range(4):
                totals = None
                for d in range(3):
                    factors = (sums[slot][s][d], shifted[slot][s][d][0], shifted[slot][s][d][1])
                    terms = [link[None] * f.reshape(3, 8, 128) for link, f in zip(links[d], factors)]
                    totals = terms if totals is None else [x + y for x, y in zip(totals, terms)]
                of_spin.append(((totals[0] - totals[2]).reshape(24, 128), (totals[0] + totals[1]).reshape(24, 128)))
            hops.append(of_spin)
        for s in range(4):
            other = SOURCE[directions[0]][s]
            k = (s % 2) * 3 + c
            k_cross = (other % 2) * 3 + c
            for q in range(2):
                both = jnp.concatenate([hops[0][s][q], hops[1][s][q]], 0).astype(jnp.bfloat16)
                right[s // 2, 48 * q:48 * q + 48, 128 * k:128 * k + 128] = both
                if other % 2 == 1:
                    both = both * flip
                right[other // 2, 96 + 48 * q:144 + 48 * q, 128 * k_cross:128 * k_cross + 128] = both


def place_left(values, edges, left):
    for s in range(4):
        for c in range(3):
            rows = []
            for part in values[s][c]:
                zero = jnp.zeros_like(part)
                rows += [part, jnp.where(edges[0], part, zero), jnp.where(edges[1], part, zero)]
            k = (s % 2) * 3 + c
            left[s // 2, :, 128 * k:128 * k + 128] = jnp.concatenate(rows, 0).astype(jnp.bfloat16)


def joined(of_re, of_im):
    return of_re[:, :72] + of_im[:, 72:], of_im[:, :72] - of_re[:, 72:]


def combine(raw, directions, chi):
    same = joined(raw[0:48], raw[48:96])
    cross = joined(raw[96:144], raw[144:192])
    rows = []
    for slot, direction in enumerate(directions):
        span = slice(24 * slot, 24 * slot + 24)
        pair = [(-same[0][span], -same[1][span]), turn(cross[0][span], cross[1][span], PHASE[direction][chi])]
        first, second = pair if chi == 0 else pair[::-1]
        rows += [first[0], second[0], first[1], second[1]]
    if raw.shape[0] == 240:
        rows += joined(raw[192:216], raw[216:240])
    return jnp.concatenate(rows, 0)


def flips(odd_slot):
    row = lax.broadcasted_iota(jnp.int32, (48, 128), 0)
    return jnp.where(row // 24 == odd_slot, -1.0, 1.0).astype(jnp.bfloat16)


def load(ref, *index):
    out = []
    for s in range(4):
        row = []
        for c in range(3):
            k = 48 * (s * 3 + c)
            whole = ref[*index, k:k + 48, :].astype(jnp.float32)
            row.append((whole[:24], whole[24:]))
        out.append(row)
    return out


def moved(move, *fields):
    return [[tuple(move(*(f[s][c][q] for f in fields)) for q in range(2)) for c in range(3)] for s in range(4)]


def product(left, right):
    return lax.dot_general(left, right, (((1,), (1,)), ((), ())), preferred_element_type=jnp.float32)


def spread_kernel(v_ref, u_ref, v_out, u_out, place):
    row = lax.broadcasted_iota(jnp.int32, (128, 1024), 0)
    col = lax.broadcasted_iota(jnp.int32, (128, 1024), 1)
    hit = row == col % 16 // 4 * LAT_X + col // 128 * 4 + col % 4
    for k in range(8):
        place[128 * k:128 * k + 128, :] = jnp.where(hit & (col % 128 // 16 == k), 1.0, 0.0).astype(jnp.bfloat16)
    for h in range(2):
        for ref, out in ((v_ref, v_out), (u_ref, u_out)):
            wide = jnp.concatenate([ref[8 * h + k] for k in range(8)], 1)
            found = jnp.dot(wide, place[...], preferred_element_type=jnp.float32)
            for a in range(8):
                part = found[:, 128 * a:128 * a + 128]
                out[a, h] = part.astype(jnp.bfloat16) if ref is v_ref else 0.5 * part


def plane_kernel(v_ref, u_ref, sums, left0, left1, right0, right1):
    lane = lax.broadcasted_iota(jnp.int32, (24, 128), 1)
    flip = flips(0)
    y_edge = lane // 4 % 4 == 3
    x_edge = lane % 4 == 3

    def ahead_y(part):
        return jnp.where(y_edge, pltpu.roll(part, 12, 1), pltpu.roll(part, 124, 1))

    def ahead_x(part, following):
        return jnp.where(x_edge, pltpu.roll(following, 3, 1), pltpu.roll(part, 127, 1))

    @pl.loop(0, 8)
    def _(a):
        after = lax.rem(a + 1, 8)
        halves = []
        for h, (left, right) in enumerate(((left0, right0), (left1, right1))):
            values = load(v_ref, a, h)
            place_left(values, (y_edge, x_edge), left)
            for s in range(4):
                for c in range(3):
                    vr, vi = values[s][c]
                    k = (s % 2) * 3 + c
                    right[s // 2, 192:240, 128 * k:128 * k + 128] = (
                        jnp.concatenate([vr, vi], 0).astype(jnp.bfloat16))
            ahead = (moved(ahead_y, values), moved(ahead_x, values, load(v_ref, after, h)))
            place_hops((2, 3), ahead, u_ref, a, h, flip, right)
            halves.append([product(right[chi], left[chi]) for chi in range(2)])
        for chi in range(2):
            raw = halves[0][chi] + halves[1][chi]
            sums[a, chi] = combine(raw, (2, 3), chi)


def line_kernel(v_ref, u_ref, face_t, face_z, place, plane_sums, blocks, stored,
                far_t, far_z, flat, left0, left1, right0, right1):
    wide = jnp.concatenate([face_t[k] for k in range(4)], 1)
    found = jnp.dot(wide, place[0:512, :], preferred_element_type=jnp.float32)
    for a in range(8):
        far_t[a] = found[:, 128 * a:128 * a + 128].astype(jnp.bfloat16)
    ends = jnp.concatenate([place[384:512, :], place[896:1024, :]], 0)
    for h in range(2):
        wide = jnp.concatenate([face_z[2 * h], face_z[2 * h + 1]], 1)
        found = jnp.dot(wide, ends, preferred_element_type=jnp.float32)
        for a in range(8):
            far_z[a, h] = found[:, 128 * a:128 * a + 128].astype(jnp.bfloat16)

    lane = lax.broadcasted_iota(jnp.int32, (24, 128), 1)
    flip = flips(1)
    upper = lane >= 64
    z_edge = lane // 16 % 4 == 3
    nowhere = lane < 0
    row = lax.broadcasted_iota(jnp.int32, (48, 48), 0)
    col = lax.broadcasted_iota(jnp.int32, (48, 48), 1)
    sign = jnp.where((row < 24) == (col < 24), 1.0, -1.0)
    zero = jnp.zeros((24, 24), jnp.float32)

    def ahead_t(part, following):
        return pltpu.roll(jnp.where(upper, part, following), 64, 1)

    def ahead_z(part, face):
        return jnp.where(z_edge, face, pltpu.roll(part, 112, 1))

    @pl.loop(0, 8)
    def _(a):
        halves = []
        for h, (left, right) in enumerate(((left0, right0), (left1, right1))):
            values = load(v_ref, a, h)
            place_left(values, (upper if h == 1 else nowhere, z_edge), left)
            following = load(v_ref, a, 1) if h == 0 else load(far_t, a)
            ahead = (moved(ahead_t, values, following), moved(ahead_z, values, load(far_z, a, h)))
            place_hops((0, 1), ahead, u_ref, a, h, flip, right)
            halves.append([product(right[chi], left[chi]) for chi in range(2)])
        line = []
        plane = []
        for chi in range(2):
            raw = halves[0][chi] + halves[1][chi]
            line.append(combine(raw, (0, 1), chi))
            plane.append(plane_sums[a, chi])

        def pick(sums, slot, kind):
            return jnp.concatenate(
                [part[96 * slot:96 * slot + 96, 24 * kind:24 * kind + 24] for part in sums], 1)

        inner = (pick(line, 0, 0) - pick(line, 0, 1)) + (pick(line, 1, 0) - pick(line, 1, 2))
        inner = inner + (pick(plane, 0, 0) - pick(plane, 0, 1)) + (pick(plane, 1, 0) - pick(plane, 1, 2))
        gram = []
        for part in range(2):
            rows = slice(192 + 24 * part, 216 + 24 * part)
            gram.append(jnp.concatenate([plane[0][rows, 0:24], zero], 1))
            gram.append(jnp.concatenate([zero, plane[1][rows, 0:24]], 1))
        whole = (inner + jnp.concatenate(gram, 0)).T
        whole = whole + jnp.concatenate([sign * inner[:48], -sign * inner[48:]], 1)
        kept = [whole, pick(line, 0, 1).T, pick(line, 1, 2).T, pick(plane, 0, 1).T, pick(plane, 1, 2).T]
        for i, block in enumerate(kept):
            blocks[a, i] = block
            flat[pl.ds(pl.multiple_of(a * 240 + i * 48, 8), 48), 0:96] = block

    for i in range(5):
        for g in range(6):
            group = [flat[pl.ds(i * 48 + g * 8 + v, 8, stride=240), :] for v in range(8)]
            stored[i, :, 384 * g:384 * g + 384] = jnp.concatenate([x[:, :48] for x in group], 1)
            stored[i, :, 2304 + 384 * g:2688 + 384 * g] = jnp.concatenate([x[:, 48:96] for x in group], 1)


def coarse_kernel(axes, blocks, phi_ref, out_ref, phi, ahead, back, got, send, recv):
    counts = [lax.axis_size(name) for name in axes]
    here = [lax.axis_index(name) for name in axes]

    def target(axis, step):
        spot = list(here)
        spot[axis] = lax.rem(here[axis] + step + counts[axis], counts[axis])
        return tuple(spot)

    barrier = pltpu.get_barrier_semaphore()
    for axis in range(2):
        for step in (-1, 1):
            pl.semaphore_signal(barrier, inc=1, device_id=target(axis, step), device_id_type=MESH)
    pl.semaphore_wait(barrier, 4)

    lane = lax.broadcasted_iota(jnp.int32, (1, 96), 1)
    row48 = lax.broadcasted_iota(jnp.int32, (48, 96), 0)
    lane48 = lax.broadcasted_iota(jnp.int32, (48, 96), 1)
    first = lane < 48
    gamma_row = jnp.where(lane % 48 < 24, 1.0, -1.0)
    gamma_col = jnp.where(lax.broadcasted_iota(jnp.int32, (48, 1), 0) < 24, 1.0, -1.0)
    eye_re = jnp.where(row48 == lane48, 1.0, 0.0)
    eye_im = jnp.where(row48 + 48 == lane48, 1.0, 0.0)

    def swapped(vector):
        return jnp.concatenate([vector[:, 48:], vector[:, :48]], 1)

    def forward(block, vector):
        other = swapped(vector)
        return block * jnp.where(first, vector, -vector), block * other

    def columns(vector):
        re = jnp.sum(vector * eye_re, 1, keepdims=True) * gamma_col
        im = jnp.sum(vector * eye_im, 1, keepdims=True) * gamma_col
        return re, im

    def backward(block, cols):
        re = jnp.sum(block * cols[0], 0, keepdims=True)
        im = jnp.sum(block * cols[1], 0, keepdims=True)
        other_im = swapped(im)
        return gamma_row * jnp.where(first, re + other_im, other_im - re)

    def copy(step, kind, src, dst, to):
        return pltpu.make_async_remote_copy(
            src_ref=src, dst_ref=dst, send_sem=send.at[step, kind], recv_sem=recv.at[step, kind],
            device_id=to, device_id_type=MESH)

    phi[0] = phi_ref[...]
    for step in range(2):
        copies = []
        for axis in range(2):
            copies.append(copy(step, axis, phi.at[step], ahead.at[step, axis], target(axis, -1)))
            copies[-1].start()
        local = [None] * 8
        cols = [columns(phi[step, a:a + 1]) for a in range(8)]
        for axis in range(2):
            for a in range(8):
                back[step, axis, a:a + 1] = backward(blocks[a, 1 + axis], cols[a])
            copies.append(copy(step, 2 + axis, back.at[step, axis], got.at[step, axis], target(axis, 1)))
            copies[-1].start()
        sums = []
        rows = []
        for a in range(8):
            own = phi[step, a:a + 1]
            right = phi[step, (a + 1) % 8:(a + 1) % 8 + 1]
            re0, im0 = forward(blocks[a, 0] + blocks[a, 3], own)
            re1, im1 = forward(blocks[a, 4], right)
            sums.append((re0 + re1, im0 + im1))
            rows.append(backward(blocks[a, 3], cols[a]) + backward(blocks[(a + 7) % 8, 4], cols[(a + 7) % 8]))
        for item in copies:
            item.wait()
        for a in range(8):
            re, im = sums[a]
            for axis in range(2):
                more_re, more_im = forward(blocks[a, 1 + axis], ahead[step, axis, a:a + 1])
                re = re + more_re
                im = im + more_im
            re = jnp.sum(re, 1, keepdims=True)
            im = jnp.sum(im, 1, keepdims=True)
            total = jnp.sum(re * eye_re + im * eye_im, 0, keepdims=True) + rows[a]
            total = total + got[step, 0, a:a + 1] + got[step, 1, a:a + 1]
            if step == 0:
                phi[1, a:a + 1] = total
            else:
                out_ref[a:a + 1] = total


def shifted_2(value, axis, steps):
    count = lax.axis_size(axis)
    pairs = [(source, (source + steps) % count) for source in range(count)]
    return lax.ppermute(value, axis, pairs)


def per_device(null_vectors, gauge_links, coarse_in):
    vectors = null_vectors.reshape(2, 24, 4, 3, 16, 128).transpose(4, 2, 3, 0, 1, 5).reshape(16, 576, 128)
    links = gauge_links.reshape(72, 16, 128).transpose(1, 0, 2)
    vmem = pl.BlockSpec(memory_space=pltpu.VMEM)
    limit = pltpu.CompilerParams(vmem_limit_bytes=24 * 1024 * 1024)
    spread_v, spread_u, place = pl.pallas_call(
        spread_kernel,
        out_shape=(
            jax.ShapeDtypeStruct((8, 2, 576, 128), jnp.bfloat16),
            jax.ShapeDtypeStruct((8, 2, 72, 128), jnp.float32),
            jax.ShapeDtypeStruct((1024, 1024), jnp.bfloat16),
        ),
        in_specs=[vmem] * 2,
        out_specs=(vmem, vmem, vmem),
        compiler_params=limit,
        cost_estimate=pl.CostEstimate(flops=2_700_000_000, bytes_accessed=7_000_000, transcendentals=0),
    )(vectors, links)
    vectors, spread_v = lax.optimization_barrier((vectors, spread_v))
    face_t = shifted_2(vectors[0:4], "ta", -1)
    face_z = shifted_2(vectors[0::4], "sa", -1)
    operands = [
        pltpu.VMEM((2, 144, 768), jnp.bfloat16),
        pltpu.VMEM((2, 144, 768), jnp.bfloat16),
    ]
    plane_sums = pl.pallas_call(
        plane_kernel,
        out_shape=jax.ShapeDtypeStruct((8, 2, 240, 72), jnp.float32),
        in_specs=[vmem] * 2,
        out_specs=vmem,
        scratch_shapes=operands + [pltpu.VMEM((2, 240, 768), jnp.bfloat16)] * 2,
        compiler_params=limit,
        cost_estimate=pl.CostEstimate(flops=8_000_000_000, bytes_accessed=4_000_000, transcendentals=0),
    )(spread_v, spread_u)
    blocks, stored = pl.pallas_call(
        line_kernel,
        out_shape=(
            jax.ShapeDtypeStruct((8, 5, 48, 96), jnp.float32),
            jax.ShapeDtypeStruct((5, 8, 4608), jnp.float32),
        ),
        in_specs=[vmem] * 6,
        out_specs=(vmem, vmem),
        scratch_shapes=[
            pltpu.VMEM((8, 576, 128), jnp.bfloat16),
            pltpu.VMEM((8, 2, 576, 128), jnp.bfloat16),
            pltpu.VMEM((1920, 128), jnp.float32),
        ] + operands + [pltpu.VMEM((2, 192, 768), jnp.bfloat16)] * 2,
        compiler_params=limit,
        cost_estimate=pl.CostEstimate(flops=8_000_000_000, bytes_accessed=6_000_000, transcendentals=0),
    )(spread_v, spread_u, face_t, face_z, place, plane_sums)
    rows = coarse_in.reshape(8, 96)
    out = pl.pallas_call(
        functools.partial(coarse_kernel, ("ta", "sa")),
        out_shape=jax.ShapeDtypeStruct((8, 96), jnp.float32),
        in_specs=[vmem] * 2,
        out_specs=vmem,
        scratch_shapes=[
            pltpu.VMEM((2, 8, 96), jnp.float32),
            pltpu.VMEM((2, 2, 8, 96), jnp.float32),
            pltpu.VMEM((2, 2, 8, 96), jnp.float32),
            pltpu.VMEM((2, 2, 8, 96), jnp.float32),
            pltpu.SemaphoreType.DMA((2, 4)),
            pltpu.SemaphoreType.DMA((2, 4)),
        ],
        compiler_params=pltpu.CompilerParams(
            collective_id=0, has_side_effects=True, vmem_limit_bytes=16 * 1024 * 1024),
    )(blocks, rows)
    stored = stored.transpose(1, 0, 2).reshape(1, 1, 8, 5, 4608)
    return stored, out.reshape(1, 1, 8, 96)


def solution(mesh):
    placed = (
        P(None, None, None, None, "ta", "sa", None),
        P(None, None, None, None, "ta", "sa", None),
        P("ta", "sa", None, None),
    )
    return jax.shard_map(
        per_device,
        mesh=mesh,
        in_specs=placed,
        out_specs=(P("ta", "sa", None, None, None), P("ta", "sa", None, None)),
        check_vma=False,
    )
```
